32 devices in a mesh: store: 4 (over z), tensor: 8 (over y, x, core).
Axes of the slice: x: 2, y: 2, z: 4, core: 2. Of those that a mesh axis runs over, the one named last changes fastest.
Arguments:
- attention_output: bfloat16 [64, 1024], P('store', 'tensor'), may hold values from -6 to 6
- residual_input: bfloat16 [64, 8192], P(('store', 'tensor')), may hold values from -6 to 6
- output_weight: bfloat16 [1024, 8192], P('tensor'), may hold values from -0.1875 to 0.1875
- query_weight: bfloat16 [8192, 1024], P(None, 'tensor'), may hold values from -0.0625 to 0.0625
- next_norm_gain: float32 [8192], replicated, may hold values from 0.1 to 1.9
- output_down_maps: bfloat16 [8, 1024, 64], P('store', 'tensor'), may hold values from -0.1875 to 0.1875
- output_up_maps: bfloat16 [8, 64, 8192], P('store', None, 'tensor'), may hold values from -0.75 to 0.75
- query_down_maps: bfloat16 [8, 8192, 64], P('store', 'tensor'), may hold values from -0.0625 to 0.0625
- query_up_maps: bfloat16 [8, 64, 1024], P('store', None, 'tensor'), may hold values from -0.75 to 0.75
- request_adapter: int32 [12], replicated, may hold values from 0 to 7
- adapter_store_slot: int32 [8], replicated, may hold values from 0 to 7, each once
- request_block_count: int32 [4, 3], P('store'), may hold values from 1 to 4, 8 in all within a row
Outputs:
- new_hidden: bfloat16 [64, 8192], P(('store', 'tensor'))
- queries: bfloat16 [64, 1024], P('store', 'tensor')
The draws below stay inside these ranges and needn't reach their ends.
Inputs may be any that keep to these rules, and one draw needn't show every extreme that they name: `request_adapter`: request i belongs to store group i // 3; any adapter may be named by several requests. `adapter_store_slot`: a permutation; slot s is held by store index s // 2 at its place s % 2. `request_block_count`: each row sums to 8, so a group's segments fill its 16 rows in request order.
All inputs are finite; a program needn't handle non-finite values.
Results may differ from the reference program's by a relative error of at most 0.015.
Values may be sent and summed in bfloat16 or wider, within the bound.
No kernel may reach another device: no remote copies, remote signals or barrier semaphores. Data moves between devices by JAX's collectives and lax.ppermute only.
A program may use at most 64 MiB of HBM per device.

```python
import math
import jax
import jax.numpy as jnp
import numpy as np
from jax import lax

HIDDEN_WIDTH = 8192
HD = 128
LOW_RANK_SIZE = 64
SP_DEV = 2
GROUP_REQUESTS = 3
QUERY_WINDOW = 1024
TOK_GRP = 16
TOKENS = 64
REQUESTS = 12
ADAPTER_TOTAL = 8
N_STORE = 4
N_TENSOR = 8


def plant(entries, key, low, top_value):
    extent = entries.shape
    index_at = [jax.random.randint(jax.random.fold_in(key, axis), (), 0, extent[axis]) for axis in range(len(extent))]
    entries = entries.at[tuple(index_at)].set(low)
    longest = extent.index(max(extent))
    index_at[longest] = (index_at[longest] + 1) % extent[longest]
    return entries.at[tuple(index_at)].set(top_value)


def levels(stream_key, shape, shards, smallest, largest):
    def one(axis_at, shards_of):
        draws = jax.random.uniform(jax.random.fold_in(jax.random.fold_in(stream_key, 6), axis_at), (shards_of,), jnp.float32, smallest / len(shards), largest / len(shards))
        return jnp.repeat(jnp.exp(draws), shape[axis_at] // shards_of).reshape((-1,) + (1,) * (len(shape) - axis_at - 1))

    gain = one(*shards[0])
    for cut in shards[1:]:
        gain = gain * one(*cut)
    return gain


def rank_table(amount, slope):
    loads = [(1 << 20) // math.isqrt(rank ** slope) + 1 for rank in range(1, amount + 1)]
    width = 1 + sum(loads) // (1 << 30)
    return np.cumsum(np.array([max(1, weight // width) for weight in loads]))


def ranked(stream_key, dims, amount, lean):
    listing = rank_table(amount, lean)
    ticket = jax.random.randint(jax.random.fold_in(stream_key, 1), dims, 0, int(listing[amount - 1]))
    standing = jnp.searchsorted(jnp.asarray(listing, jnp.int32), ticket, side="right")
    return jax.random.permutation(jax.random.fold_in(stream_key, 2), amount)[standing].astype(jnp.int32)


def profile(count, total, bound, skew):
    portions = [(1 << 20) // math.isqrt(rank ** skew) + 1 for rank in range(2, count + 1)]
    spare, counts = total - bound - (count - 1), [1] * (count - 1)
    while spare > 0:
        free = [i for i in range(count - 1) if counts[i] < bound]
        pool, remaining = sum([portions[i] for i in free]), spare
        for i in free:
            addition = min(bound - counts[i], max(1, remaining * portions[i] // pool), spare)
            counts[i] = counts[i] + addition
            spare = spare - addition
    return np.array([bound] + counts)


def uneven(key, number_of, total, reach, skew):
    if number_of == 2:
        one = jax.random.randint(key, (), max(1, total - reach), min(reach, total - 1) + 1)
        return jnp.stack([one, total - one])
    lengths = jnp.asarray(profile(number_of, total, reach, skew), jnp.int32)
    twos = (number_of - 1) // 2
    source_of, sink = lengths[1:1 + 2 * twos:2], lengths[2:2 + 2 * twos:2]
    margin = jnp.minimum(source_of - 1, reach - sink)
    shifted = jax.random.randint(jax.random.fold_in(key, 1), (twos,), 0, 1 << 20) % (margin + 1)
    lengths = lengths.at[1:1 + 2 * twos:2].set(source_of - shifted).at[2:2 + 2 * twos:2].set(sink + shifted)
    return lengths[jax.random.permutation(jax.random.fold_in(key, 2), number_of)]


def noise(stream_key, extent, deviation, limit, cuts=(), held_as=jnp.bfloat16):
    array = deviation * jax.random.normal(stream_key, extent, jnp.float32)
    if cuts:
        array = array * levels(stream_key, extent, cuts, -0.22, 0.18)
    return jnp.clip(array, -limit, limit).astype(held_as)


def setup_inputs(seed: int = 0) -> dict:
    arg_keys = jax.random.split(jax.random.key(seed), 13)
    return {
        "attention_output": noise(arg_keys[0], (TOKENS, QUERY_WINDOW), 1.0, 6.0, ((0, 4), (1, 8))),
        "residual_input": noise(arg_keys[1], (TOKENS, HIDDEN_WIDTH), 1.0, 6.0, ((0, 32),)),
        "output_weight": noise(arg_keys[2], (QUERY_WINDOW, HIDDEN_WIDTH), QUERY_WINDOW ** -0.5, 0.1875, ((0, 8),)),
        "query_weight": noise(arg_keys[3], (HIDDEN_WIDTH, QUERY_WINDOW), HIDDEN_WIDTH ** -0.5, 0.0625, ((1, 8),)),
        "next_norm_gain": jnp.clip(1.0 + 0.18 * jax.random.normal(arg_keys[4], (HIDDEN_WIDTH,), jnp.float32), 0.1, 1.9),
        "output_down_maps": noise(arg_keys[5], (ADAPTER_TOTAL, QUERY_WINDOW, LOW_RANK_SIZE), QUERY_WINDOW ** -0.5, 0.1875, ((0, 4), (1, 8))),
        "output_up_maps": noise(arg_keys[6], (ADAPTER_TOTAL, LOW_RANK_SIZE, HIDDEN_WIDTH), LOW_RANK_SIZE ** -0.5, 0.75, ((0, 4), (2, 8))),
        "query_down_maps": noise(arg_keys[7], (ADAPTER_TOTAL, HIDDEN_WIDTH, LOW_RANK_SIZE), HIDDEN_WIDTH ** -0.5, 0.0625, ((0, 4), (1, 8))),
        "query_up_maps": noise(arg_keys[8], (ADAPTER_TOTAL, LOW_RANK_SIZE, QUERY_WINDOW), LOW_RANK_SIZE ** -0.5, 0.75, ((0, 4), (2, 8))),
        "request_adapter": plant(ranked(arg_keys[9], (REQUESTS,), ADAPTER_TOTAL, 2), jax.random.fold_in(arg_keys[9], 3), 0, ADAPTER_TOTAL - 1).astype(jnp.int32),
        "adapter_store_slot": jax.random.permutation(arg_keys[10], ADAPTER_TOTAL).astype(jnp.int32),
        "request_block_count": jax.vmap(lambda own: uneven(own, GROUP_REQUESTS, N_TENSOR, N_TENSOR // 2, 2))(jax.random.split(arg_keys[11], N_STORE)).reshape((N_STORE, GROUP_REQUESTS)).astype(jnp.int32),
    }


adapter_factor = 0.5

def segment_masks(request_block_count):
    seg_ends = jnp.cumsum(request_block_count, axis=1, dtype=jnp.int32) * SP_DEV
    seg_starts = seg_ends - request_block_count * SP_DEV
    row_index = jnp.arange(TOK_GRP, dtype=jnp.int32)
    inside = (row_index[None, :, None] >= seg_starts[:, None, :]) & (row_index[None, :, None] < seg_ends[:, None, :])
    return inside.astype(jnp.float32)

def select_rows(partial_pieces, request_row_mask):
    return lax.optimization_barrier(jnp.sum(partial_pieces * request_row_mask[:, :, None], axis=1))

def expand_token_mask(shrunk, request_row_mask):
    return (shrunk.astype(jnp.float32)[:, None, :] * request_row_mask[:, :, None]).reshape(shrunk.shape[0], -1)

def reference(attention_output, residual_input, output_weight, query_weight, next_norm_gain, output_down_maps, output_up_maps, query_down_maps, query_up_maps, request_adapter, adapter_store_slot, request_block_count):
    slot_table = adapter_store_slot[request_adapter].reshape(N_STORE, GROUP_REQUESTS)
    all_masks = segment_masks(request_block_count)
    attention = attention_output.reshape(N_STORE, TOK_GRP, QUERY_WINDOW)
    residual = residual_input.reshape(N_STORE, TOK_GRP, HIDDEN_WIDTH)
    owned_width = HIDDEN_WIDTH // N_TENSOR
    column_owner = jnp.arange(HIDDEN_WIDTH, dtype=jnp.int32) // owned_width

    def one_group(inputs):
        acts, stream, local_store_slots, request_row_mask = inputs
        output_down_part = output_down_maps[local_store_slots].astype(jnp.float32)
        output_raise_piece = output_up_maps[local_store_slots].astype(jnp.float32)
        query_down_part = query_down_maps[local_store_slots].astype(jnp.float32)
        query_up_part = query_up_maps[local_store_slots].astype(jnp.float32)
        parts_o = jnp.einsum('tk,jkr->tjr', acts.astype(jnp.float32), output_down_part)
        output_combined = select_rows(parts_o, request_row_mask).astype(jnp.bfloat16)
        low_rank_output = adapter_factor * jnp.dot(expand_token_mask(output_combined, request_row_mask), output_raise_piece.reshape(GROUP_REQUESTS * LOW_RANK_SIZE, HIDDEN_WIDTH))

        def head_term(running, head_index):
            head_acts = lax.dynamic_slice_in_dim(acts, head_index * HD, HD, 1)
            head_rows = lax.dynamic_slice_in_dim(output_weight, head_index * HD, HD, 0)
            value_fraction = jnp.dot(head_acts, head_rows, preferred_element_type=jnp.float32)
            held_locally = (column_owner == head_index).astype(jnp.float32)
            value_fraction = value_fraction + low_rank_output * held_locally[None, :]
            rounded = lax.optimization_barrier(value_fraction.astype(jnp.bfloat16))
            return (running + rounded.astype(jnp.float32), None)
        projected_output, _ = lax.scan(head_term, jnp.zeros((TOK_GRP, HIDDEN_WIDTH), jnp.float32), jnp.arange(N_TENSOR, dtype=jnp.int32))
        new_hidden = (stream.astype(jnp.float32) + projected_output).astype(jnp.bfloat16)
        widened = new_hidden.astype(jnp.float32)
        scale_rows = lax.rsqrt(lax.optimization_barrier(jnp.mean(widened * widened, axis=1, keepdims=True)) + 1e-05)
        normed = (widened * scale_rows * next_norm_gain[None, :]).astype(jnp.bfloat16)
        parts_q = jnp.einsum('td,jdr->tjr', normed.astype(jnp.float32), query_down_part)
        query_reduced = select_rows(parts_q, request_row_mask).astype(jnp.bfloat16)
        queries = jnp.dot(normed, query_weight, preferred_element_type=jnp.float32)
        queries = queries + adapter_factor * jnp.dot(expand_token_mask(query_reduced, request_row_mask), query_up_part.reshape(GROUP_REQUESTS * LOW_RANK_SIZE, QUERY_WINDOW))
        return (new_hidden, queries.astype(jnp.bfloat16))
    new_hidden, queries = lax.map(one_group, (attention, residual, slot_table, all_masks))
    return (new_hidden.reshape(TOKENS, HIDDEN_WIDTH), queries.reshape(TOKENS, QUERY_WINDOW))
```

```python
import functools

import jax
import jax.numpy as jnp
from jax import lax
from jax.experimental import pallas as pl
from jax.experimental.pallas import tpu as pltpu
from jax.sharding import PartitionSpec as P

adapter_factor = 0.5
LANES = 128
SMEM = pl.BlockSpec(memory_space=pltpu.SMEM)
VMEM = pl.BlockSpec(memory_space=pltpu.VMEM)
bf16, f32 = jnp.bfloat16, jnp.float32


def params(**kw):
    return pltpu.CompilerParams(vmem_limit_bytes=48 * 2**20, **kw)


def rows_dot_rows(a, b):
    return lax.dot_general(a, b, (((1,), (1,)), ((), ())), preferred_element_type=f32)


def pack_rows(requests, sp_rows, at, adapter_of, slot_of, counts, attention, out):
    rows, head = attention.shape
    row = lax.broadcasted_iota(jnp.int32, (rows, LANES), 0)
    slots = jnp.zeros((rows, LANES), jnp.int32)
    start = jnp.int32(0)
    for j in range(requests):
        end = start + counts[0, j] * sp_rows
        slot = slot_of[adapter_of[at[0] * requests + j]]
        slots = jnp.where((row >= start) & (row < end), slot, slots)
        start = end
    out[:, :head] = attention[...]
    out[:, head:] = slots.astype(f32).astype(bf16)


def own_mask(packed, head, first_slot, rank):
    slots = packed[:, head:].astype(f32).astype(jnp.int32)
    lane = lax.broadcasted_iota(jnp.int32, slots.shape, 1)
    return slots == first_slot + lane // rank


def base_rows(at, attention, weight, residual, out):
    total = jnp.dot(attention[...], weight[...], preferred_element_type=f32)
    sp_rows = residual.shape[0]
    row = lax.broadcasted_iota(jnp.int32, total.shape, 0)
    kept = residual[...].astype(f32)
    for i in range(sp_rows):
        total = total + jnp.where(row == at[1] * sp_rows + i, kept[i : i + 1], 0.0)
    out[0] = total.astype(bf16)


def shrink_and_pack(stores, adapters, rank, at, base, down, *refs):
    packed, out = refs[:stores], refs[stores]
    tensors, rows, piece = base.shape
    head = down.shape[1]
    for r in range(stores):
        shrunk = rows_dot_rows(packed[r][:, :head], down[...])
        shrunk = jnp.where(own_mask(packed[r], head, at[0] * adapters, rank), shrunk, 0.0)
        shrunk = shrunk.astype(bf16)
        for t in range(tensors):
            out[t, :, piece + r * LANES : piece + (r + 1) * LANES] = shrunk
    for t in range(tensors):
        out[t, :, :piece] = base[t]


def sum_and_raise(stores, piece, received, up, own, *sent):
    tensors = received.shape[0]
    total = received[0].astype(f32)
    for t in range(1, tensors):
        total = total + received[t].astype(f32)
    base = total[:, :piece]
    rows = base.shape[0]
    for r in range(stores):
        shrunk = total[:, piece + r * LANES : piece + (r + 1) * LANES].astype(bf16)
        lora = adapter_factor * jnp.dot(shrunk, up[...], preferred_element_type=f32)
        if r == 0:
            own[...] = base + lora
        else:
            sent[r - 1][:rows] = base.astype(bf16)
            sent[r - 1][rows:] = lora.astype(bf16)


def hidden_and_shrink(stores, adapters, rank, head, at, own, gain, down, *refs):
    n = stores - 1
    sent, came, packed, out = refs[:n], refs[n : 2 * n], refs[2 * n : 2 * n + stores], refs[-1]
    rows, piece = own.shape
    mine = own[...]
    for r in range(n):
        mine = mine + came[r][rows:].astype(f32)
    hidden = mine.astype(bf16)
    out[:, :piece] = hidden
    gains = gain[at[1]]
    for r in range(stores):
        if r == 0:
            wide = hidden.astype(f32)
        else:
            wide = came[r - 1][:rows].astype(f32) + sent[r - 1][rows:].astype(f32)
        shrunk = rows_dot_rows((wide * gains).astype(bf16), down[...])
        shrunk = jnp.where(own_mask(packed[r], head, at[0] * adapters, rank), shrunk, 0.0)
        out[:, piece + r * LANES : piece + (r + 1) * LANES] = shrunk.astype(bf16)


def raise_queries(stores, piece, gathered, up, *out):
    tensors = gathered.shape[0]
    for r in range(stores):
        columns = slice(piece + r * LANES, piece + (r + 1) * LANES)
        shrunk = gathered[0, :, columns].astype(f32)
        for t in range(1, tensors):
            shrunk = shrunk + gathered[t, :, columns].astype(f32)
        raised = adapter_factor * jnp.dot(shrunk.astype(bf16), up[...], preferred_element_type=f32)
        out[r][...] = raised.astype(out[r].dtype)


def base_queries(width, at, gathered, gain, weight, raised, hidden, base, scale, total, squares):
    k = pl.program_id(0)
    piece = weight.shape[0]
    sp_rows = hidden.shape[0]

    @pl.when(k == 0)
    def _():
        total[...] = jnp.zeros_like(total)
        squares[...] = jnp.zeros_like(squares)

    wide = gathered[0, :, :piece].astype(f32)
    squares[...] += jnp.broadcast_to(jnp.sum(wide * wide, axis=1, keepdims=True), squares.shape)
    total[...] += jnp.dot((wide * gain[0]).astype(bf16), weight[...], preferred_element_type=f32)
    row = lax.broadcasted_iota(jnp.int32, wide.shape, 0)
    for i in range(sp_rows):
        picked = jnp.where(row == at[1] * sp_rows + i, wide, 0.0)
        hidden[i : i + 1] = jnp.sum(picked, axis=0, keepdims=True).astype(bf16)

    @pl.when(k == pl.num_programs(0) - 1)
    def _():
        s = lax.rsqrt(squares[...] / width + 1e-05)
        scale[...] = s
        base[...] = s * (total[...] + raised[...])


def on_device(
    attention_output,
    residual_input,
    output_weight,
    query_weight,
    next_norm_gain,
    output_down_maps,
    output_up_maps,
    query_down_maps,
    query_up_maps,
    request_adapter,
    adapter_store_slot,
    request_block_count,
):
    stores, tensors = lax.axis_size("store"), lax.axis_size("tensor")
    rows, head = attention_output.shape
    sp_rows, width = residual_input.shape
    requests = request_block_count.shape[1]
    adapters, _, rank = output_down_maps.shape
    piece = output_up_maps.shape[2]
    queries_here = query_weight.shape[1]
    pairs = adapters * rank
    at = jnp.stack([lax.axis_index("store"), lax.axis_index("tensor")]).astype(jnp.int32)
    down_o = output_down_maps.transpose(0, 2, 1).reshape(pairs, head)
    up_o = output_up_maps.reshape(pairs, piece)
    down_q = query_down_maps.transpose(0, 2, 1).reshape(pairs, piece)
    up_q = query_up_maps.reshape(pairs, queries_here)
    gain = next_norm_gain.reshape(tensors, 1, piece)
    message = piece + stores * LANES

    def across_stores(arrays):
        return [
            lax.ppermute(a, "store", [(i, i ^ (r + 1)) for i in range(stores)])
            for r, a in enumerate(arrays)
        ]

    packed0 = pl.pallas_call(
        functools.partial(pack_rows, requests, sp_rows),
        out_shape=jax.ShapeDtypeStruct((rows, head + LANES), bf16),
        in_specs=[SMEM, SMEM, SMEM, SMEM, VMEM],
        out_specs=VMEM,
        name="pack_rows",
    )(at, request_adapter, adapter_store_slot, request_block_count, attention_output)
    packed = [packed0] + across_stores([packed0] * (stores - 1))

    base = pl.pallas_call(
        base_rows,
        grid=(tensors,),
        out_shape=jax.ShapeDtypeStruct((tensors, rows, piece), bf16),
        in_specs=[
            SMEM,
            pl.BlockSpec((rows, head), lambda t: (0, 0)),
            pl.BlockSpec((head, piece), lambda t: (0, t)),
            pl.BlockSpec((sp_rows, piece), lambda t: (0, t)),
        ],
        out_specs=pl.BlockSpec((1, rows, piece), lambda t: (t, 0, 0)),
        compiler_params=params(),
        cost_estimate=pl.CostEstimate(
            flops=2 * rows * head * width, bytes_accessed=2 * head * width, transcendentals=0
        ),
        name="base_rows",
    )(at, attention_output, output_weight, residual_input)

    to_peers = pl.pallas_call(
        functools.partial(shrink_and_pack, stores, adapters, rank),
        out_shape=jax.ShapeDtypeStruct((tensors, rows, message), bf16),
        in_specs=[SMEM] + [VMEM] * (2 + stores),
        out_specs=VMEM,
        compiler_params=params(),
        name="shrink_and_pack",
    )(at, base, down_o, *packed)
    received = lax.all_to_all(to_peers, "tensor", 0, 0)

    own, *sent = pl.pallas_call(
        functools.partial(sum_and_raise, stores, piece),
        out_shape=[jax.ShapeDtypeStruct((rows, piece), f32)]
        + [jax.ShapeDtypeStruct((2 * rows, piece), bf16)] * (stores - 1),
        in_specs=[VMEM] * 2,
        out_specs=[VMEM] * stores,
        compiler_params=params(),
        name="sum_and_raise",
    )(received, up_o)
    came = across_stores(sent)

    mine = pl.pallas_call(
        functools.partial(hidden_and_shrink, stores, adapters, rank, head),
        out_shape=jax.ShapeDtypeStruct((rows, message), bf16),
        in_specs=[SMEM] + [VMEM] * (3 + 2 * (stores - 1) + stores),
        out_specs=VMEM,
        compiler_params=params(),
        name="hidden_and_shrink",
    )(at, own, gain, down_q, *sent, *came, *packed)
    gathered = lax.all_gather(mine, "tensor", axis=0)

    raised, *give = pl.pallas_call(
        functools.partial(raise_queries, stores, piece),
        out_shape=[jax.ShapeDtypeStruct((rows, queries_here), f32)]
        + [jax.ShapeDtypeStruct((rows, queries_here), bf16)] * (stores - 1),
        in_specs=[VMEM] * 2,
        out_specs=[VMEM] * stores,
        compiler_params=params(),
        name="raise_queries",
    )(gathered, up_q)
    got = across_stores(give)

    new_hidden, base_q, scale = pl.pallas_call(
        functools.partial(base_queries, width),
        grid=(tensors,),
        out_shape=[
            jax.ShapeDtypeStruct((sp_rows, width), bf16),
            jax.ShapeDtypeStruct((rows, queries_here), f32),
            jax.ShapeDtypeStruct((rows, queries_here), f32),
        ],
        in_specs=[
            SMEM,
            pl.BlockSpec((1, rows, message), lambda k: (k, 0, 0)),
            pl.BlockSpec((1, 1, piece), lambda k: (k, 0, 0)),
            pl.BlockSpec((piece, queries_here), lambda k: (k, 0)),
            pl.BlockSpec((rows, queries_here), lambda k: (0, 0)),
        ],
        out_specs=[
            pl.BlockSpec((sp_rows, piece), lambda k: (0, k)),
            pl.BlockSpec((rows, queries_here), lambda k: (0, 0)),
            pl.BlockSpec((rows, queries_here), lambda k: (0, 0)),
        ],
        scratch_shapes=[pltpu.VMEM((rows, queries_here), f32), pltpu.VMEM((rows, queries_here), f32)],
        compiler_params=params(),
        cost_estimate=pl.CostEstimate(
            flops=2 * rows * width * queries_here,
            bytes_accessed=2 * width * queries_here,
            transcendentals=0,
        ),
        name="base_queries",
    )(at, gathered, gain, query_weight, raised)
    queries = base_q + scale * sum(g.astype(f32) for g in got)
    return new_hidden, queries.astype(bf16)


def solution(mesh):
    in_specs = (
        P("store", "tensor"),
        P(("store", "tensor"), None),
        P("tensor", None),
        P(None, "tensor"),
        P(),
        P("store", "tensor", None),
        P("store", None, "tensor"),
        P("store", "tensor", None),
        P("store", None, "tensor"),
        P(),
        P(),
        P("store", None),
    )
    out_specs = (P(("store", "tensor"), None), P("store", "tensor"))
    return jax.shard_map(
        on_device, mesh=mesh, in_specs=in_specs, out_specs=out_specs, check_vma=False
    )
```

```python
import functools

import jax
import jax.numpy as jnp
from jax import lax
from jax.experimental import pallas as pl
from jax.experimental.pallas import tpu as pltpu
from jax.sharding import PartitionSpec as P

adapter_factor = 0.5
LANES = 128
SMEM = pl.BlockSpec(memory_space=pltpu.SMEM)
VMEM = pl.BlockSpec(memory_space=pltpu.VMEM)
HBM = pl.BlockSpec(memory_space=pltpu.HBM)
bf16, f32 = jnp.bfloat16, jnp.float32


def params(**kw):
    return pltpu.CompilerParams(vmem_limit_bytes=48 * 2**20, **kw)


def rows_dot_rows(a, b):
    return lax.dot_general(a, b, (((1,), (1,)), ((), ())), preferred_element_type=f32)


def place():
    return lax.axis_index("store"), lax.axis_index("tensor")


def pack_rows(requests, sp_rows, counts, attention, out, count, loaded, done):
    first = pltpu.make_async_copy(counts, count, done.at[0])
    second = pltpu.make_async_copy(attention, loaded, done.at[1])
    first.start()
    second.start()
    rows, head = loaded.shape
    row = lax.broadcasted_iota(jnp.int32, (rows, LANES), 0)
    owner = jnp.zeros((rows, LANES), f32)
    first.wait()
    end = jnp.int32(0)
    for j in range(requests - 1):
        end = end + count[0, j] * sp_rows
        owner = owner + jnp.where(row >= end, 1.0, 0.0)
    out[:, head:] = owner.astype(bf16)
    second.wait()
    out[:, :head] = loaded[...]


def base_rows(
    stores, requests, adapters, rank, adapters_in, slots_in, attention, weight, residual,
    out, match, adapter_of, slot_of, acts, kept_rows, held, done,
):
    tensors, rows, piece = out.shape
    sp_rows = residual.shape[0]
    store, me = place()
    small = [
        pltpu.make_async_copy(attention, acts, done.at[tensors]),
        pltpu.make_async_copy(residual, kept_rows, done.at[tensors + 1]),
        pltpu.make_async_copy(adapters_in, adapter_of, done.at[tensors + 2]),
        pltpu.make_async_copy(slots_in, slot_of, done.at[tensors + 3]),
    ]
    for copy in small:
        copy.start()
    copies = [
        pltpu.make_async_copy(weight.at[:, pl.ds(t * piece, piece)], held.at[t], done.at[t])
        for t in range(tensors)
    ]
    for copy in copies:
        copy.start()
    for copy in small:
        copy.wait()
    lane_slot = store * adapters + lax.broadcasted_iota(jnp.int32, (1, LANES), 1) // rank
    for r in range(stores):
        for j in range(requests):
            slot = slot_of[adapter_of[(store ^ r) * requests + j]]
            i = r * requests + j
            match[i : i + 1] = jnp.where(lane_slot == slot, 1.0, 0.0)
    row = lax.broadcasted_iota(jnp.int32, (rows, piece), 0)
    for t in range(tensors):
        kept = kept_rows[:, t * piece : (t + 1) * piece].astype(f32)
        copies[t].wait()
        total = jnp.dot(acts[...], held[t], preferred_element_type=f32)
        for i in range(sp_rows):
            total = total + jnp.where(row == me * sp_rows + i, kept[i : i + 1], 0.0)
        out[t] = total.astype(bf16)


def shrink_and_pack(stores, requests, base, match, down, *refs):
    packed, (keep, give, masks) = refs[:stores], refs[stores:]
    _, rows, piece = base.shape
    head = down.shape[1]
    pieces = []
    for r in range(stores):
        owner = packed[r][:, head:].astype(f32)
        mask = jnp.zeros((rows, LANES), f32)
        for j in range(requests):
            i = r * requests + j
            mask = mask + jnp.where(owner == j, match[i : i + 1], 0.0)
        masks[r] = mask
        pieces.append((rows_dot_rows(packed[r][:, :head], down[...]) * mask).astype(bf16))
    shrunk = jnp.concatenate(pieces, axis=1)
    me = lax.axis_index("tensor")
    for c in range(keep.shape[0]):
        for out, t in ((keep, me ^ (2 * c)), (give, me ^ (2 * c + 1))):
            out[c, :, :piece] = base[t]
            out[c, :, piece:] = shrunk


def halve(keep, got, own, *sent):
    own[...] = keep[0].astype(f32) + got[0].astype(f32)
    for c, out in enumerate(sent):
        out[...] = (keep[c + 1].astype(f32) + got[c + 1].astype(f32)).astype(bf16)


def sum_and_raise(stores, piece, chips, up, half, *refs):
    came, (own, *sent) = refs[: chips - 1], refs[chips - 1 :]
    total = half[...]
    for c in came:
        total = total + c[...].astype(f32)
    base = total[:, :piece]
    rows = base.shape[0]
    for r in range(stores):
        shrunk = total[:, piece + r * LANES : piece + (r + 1) * LANES].astype(bf16)
        lora = adapter_factor * jnp.dot(shrunk, up[...], preferred_element_type=f32)
        if r == 0:
            own[...] = base + lora
        else:
            sent[r - 1][:rows] = base.astype(bf16)
            sent[r - 1][rows:] = lora.astype(bf16)


def hidden_and_shrink(stores, own, masks, gain, down, *refs):
    n = stores - 1
    sent, came, out = refs[:n], refs[n : 2 * n], refs[-1]
    rows, piece = own.shape
    mine = own[...]
    for r in range(n):
        mine = mine + came[r][rows:].astype(f32)
    hidden = mine.astype(bf16)
    out[:, :piece] = hidden
    gains = gain[lax.axis_index("tensor")]
    for r in range(stores):
        if r == 0:
            wide = hidden.astype(f32)
        else:
            wide = came[r - 1][:rows].astype(f32) + sent[r - 1][rows:].astype(f32)
        shrunk = rows_dot_rows((wide * gains).astype(bf16), down[...]) * masks[r]
        out[:, piece + r * LANES : piece + (r + 1) * LANES] = shrunk.astype(bf16)


def raise_queries(stores, tensors, piece, up, *refs):
    blocks, out = refs[:tensors], refs[tensors:]
    for r in range(stores):
        columns = slice(piece + r * LANES, piece + (r + 1) * LANES)
        shrunk = blocks[0][:, columns].astype(f32)
        for block in blocks[1:]:
            shrunk = shrunk + block[:, columns].astype(f32)
        raised = adapter_factor * jnp.dot(shrunk.astype(bf16), up[...], preferred_element_type=f32)
        out[r][...] = raised.astype(out[r].dtype)


def base_queries(tensors, gain, weight, raised, *refs):
    blocks, (hidden, base, scale) = refs[:tensors], refs[tensors:]
    sp_rows, width = hidden.shape
    piece = width // tensors
    rows = base.shape[0]
    me = lax.axis_index("tensor")
    total = jnp.zeros(base.shape, f32)
    squares = jnp.zeros((rows, 1), f32)
    row = lax.broadcasted_iota(jnp.int32, (rows, piece), 0)
    for i in range(tensors):
        k = me ^ i
        at = pl.multiple_of(k * piece, piece)
        wide = blocks[i][:, :piece].astype(f32)
        squares = squares + jnp.sum(wide * wide, axis=1, keepdims=True)
        total = total + jnp.dot(
            (wide * gain[k]).astype(bf16), weight[pl.ds(at, piece)], preferred_element_type=f32
        )
        picked = [
            jnp.sum(jnp.where(row == me * sp_rows + j, wide, 0.0), axis=0, keepdims=True)
            for j in range(sp_rows)
        ]
        hidden[:, pl.ds(at, piece)] = jnp.concatenate(picked, axis=0).astype(bf16)
    s = jnp.broadcast_to(lax.rsqrt(squares / width + 1e-05), base.shape)
    scale[...] = s
    base[...] = s * (total + raised[...])


def on_device(
    attention_output,
    residual_input,
    output_weight,
    query_weight,
    next_norm_gain,
    output_down_maps,
    output_up_maps,
    query_down_maps,
    query_up_maps,
    request_adapter,
    adapter_store_slot,
    request_block_count,
):
    stores, tensors = lax.axis_size("store"), lax.axis_size("tensor")
    rows, head = attention_output.shape
    sp_rows, width = residual_input.shape
    requests = request_block_count.shape[1]
    adapters, _, rank = output_down_maps.shape
    piece = output_up_maps.shape[2]
    queries_here = query_weight.shape[1]
    pairs, chips = adapters * rank, tensors // 2
    down_o = output_down_maps.transpose(0, 2, 1).reshape(pairs, head)
    up_o = output_up_maps.reshape(pairs, piece)
    down_q = query_down_maps.transpose(0, 2, 1).reshape(pairs, piece)
    up_q = query_up_maps.reshape(pairs, queries_here)
    gain = next_norm_gain.reshape(tensors, 1, piece)
    message = piece + stores * LANES

    def swap(a, axis, bits):
        return lax.ppermute(a, axis, [(i, i ^ bits) for i in range(lax.axis_size(axis))])

    def kernel(body, out, name, in_specs, **kw):
        return pl.pallas_call(
            body,
            out_shape=[jax.ShapeDtypeStruct(*o) for o in out],
            in_specs=in_specs,
            out_specs=[VMEM] * len(out),
            name=name,
            compiler_params=params(),
            **kw,
        )

    def stay(a):
        return pltpu.with_memory_space_constraint(a, pltpu.HBM)

    [packed0] = kernel(
        functools.partial(pack_rows, requests, sp_rows),
        [((rows, head + LANES), bf16)],
        "pack_rows",
        [HBM, HBM],
        scratch_shapes=[
            pltpu.SMEM((1, requests), jnp.int32),
            pltpu.VMEM((rows, head), bf16),
            pltpu.SemaphoreType.DMA((2,)),
        ],
    )(stay(request_block_count), stay(attention_output))
    packed = [packed0] + [swap(packed0, "store", r) for r in range(1, stores)]

    base, match = kernel(
        functools.partial(base_rows, stores, requests, adapters, rank),
        [((tensors, rows, piece), bf16), ((stores * requests, LANES), f32)],
        "base_rows",
        [HBM] * 5,
        scratch_shapes=[
            pltpu.SMEM(request_adapter.shape, jnp.int32),
            pltpu.SMEM(adapter_store_slot.shape, jnp.int32),
            pltpu.VMEM((rows, head), bf16),
            pltpu.VMEM((sp_rows, width), bf16),
            pltpu.VMEM((tensors, head, piece), bf16),
            pltpu.SemaphoreType.DMA((tensors + 4,)),
        ],
        cost_estimate=pl.CostEstimate(
            flops=2 * rows * head * width, bytes_accessed=2 * head * width, transcendentals=0
        ),
    )(
        stay(request_adapter),
        stay(adapter_store_slot),
        stay(attention_output),
        stay(output_weight),
        stay(residual_input),
    )

    keep, give, masks = kernel(
        functools.partial(shrink_and_pack, stores, requests),
        [((chips, rows, message), bf16)] * 2 + [((stores, rows, LANES), f32)],
        "shrink_and_pack",
        [VMEM] * (3 + stores),
    )(base, match, down_o, *packed)
    got = swap(give, "tensor", 1)
    half, *halves = kernel(
        halve,
        [((rows, message), f32)] + [((rows, message), bf16)] * (chips - 1),
        "halve",
        [VMEM] * 2,
    )(keep, got)
    pieces = [swap(h, "tensor", 2 * (c + 1)) for c, h in enumerate(halves)]

    own, *sent = kernel(
        functools.partial(sum_and_raise, stores, piece, chips),
        [((rows, piece), f32)] + [((2 * rows, piece), bf16)] * (stores - 1),
        "sum_and_raise",
        [VMEM] * (1 + chips),
    )(up_o, half, *pieces)
    came = [swap(a, "store", r + 1) for r, a in enumerate(sent)]

    [mine] = kernel(
        functools.partial(hidden_and_shrink, stores),
        [((rows, message), bf16)],
        "hidden_and_shrink",
        [VMEM] * (4 + 2 * (stores - 1)),
    )(own, masks, gain, down_q, *sent, *came)
    even = [mine] + [swap(mine, "tensor", 2 * c) for c in range(1, chips)]
    blocks = [b for e in even for b in (e, swap(e, "tensor", 1))]

    raised, *back = kernel(
        functools.partial(raise_queries, stores, tensors, piece),
        [((rows, queries_here), f32)] + [((rows, queries_here), bf16)] * (stores - 1),
        "raise_queries",
        [VMEM] * (1 + tensors),
    )(up_q, *blocks)
    returned = [swap(a, "store", r + 1) for r, a in enumerate(back)]

    new_hidden, base_q, scale = kernel(
        functools.partial(base_queries, tensors),
        [((sp_rows, width), bf16)] + [((rows, queries_here), f32)] * 2,
        "base_queries",
        [VMEM] * (3 + tensors),
        cost_estimate=pl.CostEstimate(
            flops=2 * rows * width * queries_here,
            bytes_accessed=2 * width * queries_here,
            transcendentals=0,
        ),
    )(gain, query_weight, raised, *blocks)
    queries = base_q + scale * sum(a.astype(f32) for a in returned)
    return new_hidden, queries.astype(bf16)


def solution(mesh):
    in_specs = (
        P("store", "tensor"),
        P(("store", "tensor"), None),
        P("tensor", None),
        P(None, "tensor"),
        P(),
        P("store", "tensor", None),
        P("store", None, "tensor"),
        P("store", "tensor", None),
        P("store", None, "tensor"),
        P(),
        P(),
        P("store", None),
    )
    out_specs = (P(("store", "tensor"), None), P("store", "tensor"))
    return jax.shard_map(
        on_device, mesh=mesh, in_specs=in_specs, out_specs=out_specs, check_vma=False
    )
```

```python
import functools

import jax
import jax.numpy as jnp
from jax import lax
from jax.experimental import pallas as pl
from jax.experimental.pallas import tpu as pltpu
from jax.sharding import PartitionSpec as P

adapter_factor = 0.5
LANES = 128
SMEM = pl.BlockSpec(memory_space=pltpu.SMEM)
VMEM = pl.BlockSpec(memory_space=pltpu.VMEM)
HBM = pl.BlockSpec(memory_space=pltpu.HBM)
bf16, f32 = jnp.bfloat16, jnp.float32


def params(**kw):
    return pltpu.CompilerParams(vmem_limit_bytes=48 * 2**20, **kw)


def rows_dot_rows(a, b):
    return lax.dot_general(a, b, (((1,), (1,)), ((), ())), preferred_element_type=f32)


def place():
    return lax.axis_index("store"), lax.axis_index("tensor")


def pack_rows(requests, sp_rows, counts, attention, out, count, loaded, done):
    first = pltpu.make_async_copy(counts, count, done.at[0])
    second = pltpu.make_async_copy(attention, loaded, done.at[1])
    first.start()
    second.start()
    rows, head = loaded.shape
    row = lax.broadcasted_iota(jnp.int32, (rows, LANES), 0)
    owner = jnp.zeros((rows, LANES), f32)
    first.wait()
    end = jnp.int32(0)
    for j in range(requests - 1):
        end = end + count[0, j] * sp_rows
        owner = owner + jnp.where(row >= end, 1.0, 0.0)
    out[:, head:] = owner.astype(bf16)
    second.wait()
    out[:, :head] = loaded[...]


def base_rows(
    stores, requests, adapters, rank, adapters_in, slots_in, attention, weight, residual,
    out, match, adapter_of, slot_of, acts, kept_rows, held, done,
):
    tensors, rows, piece = out.shape
    sp_rows = residual.shape[0]
    store, me = place()
    small = [
        pltpu.make_async_copy(attention, acts, done.at[tensors]),
        pltpu.make_async_copy(residual, kept_rows, done.at[tensors + 1]),
        pltpu.make_async_copy(adapters_in, adapter_of, done.at[tensors + 2]),
        pltpu.make_async_copy(slots_in, slot_of, done.at[tensors + 3]),
    ]
    for copy in small:
        copy.start()
    copies = [
        pltpu.make_async_copy(weight.at[:, pl.ds(t * piece, piece)], held.at[t], done.at[t])
        for t in range(tensors)
    ]
    for copy in copies:
        copy.start()
    for copy in small:
        copy.wait()
    lane_slot = store * adapters + lax.broadcasted_iota(jnp.int32, (1, LANES), 1) // rank
    for r in range(stores):
        for j in range(requests):
            slot = slot_of[adapter_of[(store ^ r) * requests + j]]
            i = r * requests + j
            match[i : i + 1] = jnp.where(lane_slot == slot, 1.0, 0.0)
    row = lax.broadcasted_iota(jnp.int32, (rows, piece), 0)
    for t in range(tensors):
        kept = kept_rows[:, t * piece : (t + 1) * piece].astype(f32)
        copies[t].wait()
        total = jnp.dot(acts[...], held[t], preferred_element_type=f32)
        for i in range(sp_rows):
            total = total + jnp.where(row == me * sp_rows + i, kept[i : i + 1], 0.0)
        out[t] = total.astype(bf16)


def shrink_and_pack(stores, requests, base, match, down, *refs):
    packed, (keep, give, masks) = refs[:stores], refs[stores:]
    _, rows, piece = base.shape
    head = down.shape[1]
    pieces = []
    for r in range(stores):
        owner = packed[r][:, head:].astype(f32)
        mask = jnp.zeros((rows, LANES), f32)
        for j in range(requests):
            i = r * requests + j
            mask = mask + jnp.where(owner == j, match[i : i + 1], 0.0)
        masks[r] = mask
        pieces.append((rows_dot_rows(packed[r][:, :head], down[...]) * mask).astype(bf16))
    shrunk = jnp.concatenate(pieces, axis=1)
    me = lax.axis_index("tensor")
    for c in range(keep.shape[0]):
        for out, t in ((keep, me ^ (2 * c)), (give, me ^ (2 * c + 1))):
            out[c, :, :piece] = base[t]
            out[c, :, piece:] = shrunk


def halve(keep, got, own, *sent):
    own[...] = keep[0].astype(f32) + got[0].astype(f32)
    for c, out in enumerate(sent[::-1]):
        out[...] = (keep[c + 1].astype(f32) + got[c + 1].astype(f32)).astype(bf16)


def sum_and_raise(stores, piece, chips, up, half, *refs):
    came, (own, *sent) = refs[: chips - 1], refs[chips - 1 :]
    sent = sent[::-1]
    total = half[...]
    for c in came:
        total = total + c[...].astype(f32)
    base = total[:, :piece]
    rows = base.shape[0]
    for r in range(stores):
        shrunk = total[:, piece + r * LANES : piece + (r + 1) * LANES].astype(bf16)
        lora = adapter_factor * jnp.dot(shrunk, up[...], preferred_element_type=f32)
        if r == 0:
            own[...] = base + lora
        else:
            sent[r - 1][:rows] = base.astype(bf16)
            sent[r - 1][rows:] = lora.astype(bf16)


def hidden_and_shrink(stores, own, masks, gain, down, *refs):
    n = stores - 1
    sent, came, out = refs[:n][::-1], refs[n : 2 * n][::-1], refs[-1]
    rows, piece = own.shape
    mine = own[...]
    for r in range(n):
        mine = mine + came[r][rows:].astype(f32)
    hidden = mine.astype(bf16)
    out[:, :piece] = hidden
    gains = gain[lax.axis_index("tensor")]
    for r in range(stores):
        if r == 0:
            wide = hidden.astype(f32)
        else:
            wide = came[r - 1][:rows].astype(f32) + sent[r - 1][rows:].astype(f32)
        shrunk = rows_dot_rows((wide * gains).astype(bf16), down[...]) * masks[r]
        out[:, piece + r * LANES : piece + (r + 1) * LANES] = shrunk.astype(bf16)


def raise_queries(stores, tensors, piece, up, *refs):
    blocks, out = refs[:tensors], refs[tensors:]
    out = out[:1] + out[:0:-1]
    for r in range(stores):
        columns = slice(piece + r * LANES, piece + (r + 1) * LANES)
        shrunk = blocks[0][:, columns].astype(f32)
        for block in blocks[1:]:
            shrunk = shrunk + block[:, columns].astype(f32)
        raised = adapter_factor * jnp.dot(shrunk.astype(bf16), up[...], preferred_element_type=f32)
        out[r][...] = raised.astype(out[r].dtype)


def base_queries(tensors, gain, weight, raised, *refs):
    blocks, (hidden, base, scale) = refs[:tensors], refs[tensors:]
    sp_rows, width = hidden.shape
    piece = width // tensors
    rows = base.shape[0]
    me = lax.axis_index("tensor")
    total = jnp.zeros(base.shape, f32)
    squares = jnp.zeros((rows, 1), f32)
    row = lax.broadcasted_iota(jnp.int32, (rows, piece), 0)
    for i in range(tensors):
        k = me ^ i
        at = pl.multiple_of(k * piece, piece)
        wide = blocks[i][:, :piece].astype(f32)
        squares = squares + jnp.sum(wide * wide, axis=1, keepdims=True)
        total = total + jnp.dot(
            (wide * gain[k]).astype(bf16), weight[pl.ds(at, piece)], preferred_element_type=f32
        )
        picked = [
            jnp.sum(jnp.where(row == me * sp_rows + j, wide, 0.0), axis=0, keepdims=True)
            for j in range(sp_rows)
        ]
        hidden[:, pl.ds(at, piece)] = jnp.concatenate(picked, axis=0).astype(bf16)
    s = jnp.broadcast_to(lax.rsqrt(squares / width + 1e-05), base.shape)
    scale[...] = s
    base[...] = s * (total + raised[...])


def on_device(
    attention_output,
    residual_input,
    output_weight,
    query_weight,
    next_norm_gain,
    output_down_maps,
    output_up_maps,
    query_down_maps,
    query_up_maps,
    request_adapter,
    adapter_store_slot,
    request_block_count,
):
    stores, tensors = lax.axis_size("store"), lax.axis_size("tensor")
    rows, head = attention_output.shape
    sp_rows, width = residual_input.shape
    requests = request_block_count.shape[1]
    adapters, _, rank = output_down_maps.shape
    piece = output_up_maps.shape[2]
    queries_here = query_weight.shape[1]
    pairs, chips = adapters * rank, tensors // 2
    down_o = output_down_maps.transpose(0, 2, 1).reshape(pairs, head)
    up_o = output_up_maps.reshape(pairs, piece)
    down_q = query_down_maps.transpose(0, 2, 1).reshape(pairs, piece)
    up_q = query_up_maps.reshape(pairs, queries_here)
    gain = next_norm_gain.reshape(tensors, 1, piece)
    message = piece + stores * LANES

    def swap(a, axis, bits):
        return lax.ppermute(a, axis, [(i, i ^ bits) for i in range(lax.axis_size(axis))])

    def kernel(body, out, name, in_specs, **kw):
        return pl.pallas_call(
            body,
            out_shape=[jax.ShapeDtypeStruct(*o) for o in out],
            in_specs=in_specs,
            out_specs=[VMEM] * len(out),
            name=name,
            compiler_params=params(),
            **kw,
        )

    def stay(a):
        return pltpu.with_memory_space_constraint(a, pltpu.HBM)

    [packed0] = kernel(
        functools.partial(pack_rows, requests, sp_rows),
        [((rows, head + LANES), bf16)],
        "pack_rows",
        [HBM, HBM],
        scratch_shapes=[
            pltpu.SMEM((1, requests), jnp.int32),
            pltpu.VMEM((rows, head), bf16),
            pltpu.SemaphoreType.DMA((2,)),
        ],
    )(stay(request_block_count), stay(attention_output))
    packed = [packed0] + [swap(packed0, "store", r) for r in range(1, stores)]

    base, match = kernel(
        functools.partial(base_rows, stores, requests, adapters, rank),
        [((tensors, rows, piece), bf16), ((stores * requests, LANES), f32)],
        "base_rows",
        [HBM] * 5,
        scratch_shapes=[
            pltpu.SMEM(request_adapter.shape, jnp.int32),
            pltpu.SMEM(adapter_store_slot.shape, jnp.int32),
            pltpu.VMEM((rows, head), bf16),
            pltpu.VMEM((sp_rows, width), bf16),
            pltpu.VMEM((tensors, head, piece), bf16),
            pltpu.SemaphoreType.DMA((tensors + 4,)),
        ],
        cost_estimate=pl.CostEstimate(
            flops=2 * rows * head * width, bytes_accessed=2 * head * width, transcendentals=0
        ),
    )(
        stay(request_adapter),
        stay(adapter_store_slot),
        stay(attention_output),
        stay(output_weight),
        stay(residual_input),
    )

    keep, give, masks = kernel(
        functools.partial(shrink_and_pack, stores, requests),
        [((chips, rows, message), bf16)] * 2 + [((stores, rows, LANES), f32)],
        "shrink_and_pack",
        [VMEM] * (3 + stores),
    )(base, match, down_o, *packed)
    got = swap(give, "tensor", 1)
    half, *halves = kernel(
        halve,
        [((rows, message), f32)] + [((rows, message), bf16)] * (chips - 1),
        "halve",
        [VMEM] * 2,
    )(keep, got)
    pieces = [swap(h, "tensor", 2 * (c + 1)) for c, h in enumerate(halves[::-1])]

    own, *sent = kernel(
        functools.partial(sum_and_raise, stores, piece, chips),
        [((rows, piece), f32)] + [((2 * rows, piece), bf16)] * (stores - 1),
        "sum_and_raise",
        [VMEM] * (1 + chips),
    )(up_o, half, *pieces[::-1])
    sent = sent[::-1]
    came = [swap(a, "store", r + 1) for r, a in enumerate(sent)]

    [mine] = kernel(
        functools.partial(hidden_and_shrink, stores),
        [((rows, message), bf16)],
        "hidden_and_shrink",
        [VMEM] * (4 + 2 * (stores - 1)),
    )(own, masks, gain, down_q, *sent[::-1], *came[::-1])
    even = [mine] + [swap(mine, "tensor", 2 * c) for c in range(1, chips)]
    blocks = [b for e in even for b in (e, swap(e, "tensor", 1))]

    raised, *back = kernel(
        functools.partial(raise_queries, stores, tensors, piece),
        [((rows, queries_here), f32)] + [((rows, queries_here), bf16)] * (stores - 1),
        "raise_queries",
        [VMEM] * (1 + tensors),
    )(up_q, *blocks)
    returned = [swap(a, "store", r + 1) for r, a in enumerate(back[::-1])]

    new_hidden, base_q, scale = kernel(
        functools.partial(base_queries, tensors),
        [((sp_rows, width), bf16)] + [((rows, queries_here), f32)] * 2,
        "base_queries",
        [VMEM] * (3 + tensors),
        cost_estimate=pl.CostEstimate(
            flops=2 * rows * width * queries_here,
            bytes_accessed=2 * width * queries_here,
            transcendentals=0,
        ),
    )(gain, query_weight, raised, *blocks)
    queries = base_q + scale * sum(a.astype(f32) for a in returned[::-1])
    return new_hidden, queries.astype(bf16)


def solution(mesh):
    in_specs = (
        P("store", "tensor"),
        P(("store", "tensor"), None),
        P("tensor", None),
        P(None, "tensor"),
        P(),
        P("store", "tensor", None),
        P("store", None, "tensor"),
        P("store", "tensor", None),
        P("store", None, "tensor"),
        P(),
        P(),
        P("store", None),
    )
    out_specs = (P(("store", "tensor"), None), P("store", "tensor"))
    return jax.shard_map(
        on_device, mesh=mesh, in_specs=in_specs, out_specs=out_specs, check_vma=False
    )
```

```python
import functools

import jax
import jax.numpy as jnp
from jax import lax
from jax.experimental import pallas as pl
from jax.experimental.pallas import tpu as pltpu
from jax.sharding import PartitionSpec as P

adapter_factor = 0.5
LANES = 128
SMEM = pl.BlockSpec(memory_space=pltpu.SMEM)
VMEM = pl.BlockSpec(memory_space=pltpu.VMEM)
HBM = pl.BlockSpec(memory_space=pltpu.HBM)
bf16, f32 = jnp.bfloat16, jnp.float32


def params(**kw):
    return pltpu.CompilerParams(vmem_limit_bytes=48 * 2**20, **kw)


def rows_dot_rows(a, b):
    return lax.dot_general(a, b, (((1,), (1,)), ((), ())), preferred_element_type=f32)


def place():
    return lax.axis_index("store"), lax.axis_index("tensor")


def pack_rows(requests, sp_rows, counts, attention, out, count, loaded, done):
    first = pltpu.make_async_copy(counts, count, done.at[0])
    second = pltpu.make_async_copy(attention, loaded, done.at[1])
    first.start()
    second.start()
    rows, head = loaded.shape
    row = lax.broadcasted_iota(jnp.int32, (rows, LANES), 0)
    owner = jnp.zeros((rows, LANES), f32)
    first.wait()
    end = jnp.int32(0)
    for j in range(requests - 1):
        end = end + count[0, j] * sp_rows
        owner = owner + jnp.where(row >= end, 1.0, 0.0)
    out[:, head:] = owner.astype(bf16)
    second.wait()
    out[:, :head] = loaded[...]


def base_rows(
    stores, requests, adapters, rank, adapters_in, slots_in, attention, weight, residual,
    out, match, adapter_of, slot_of, acts, kept_rows, held, done,
):
    tensors, rows, piece = out.shape
    sp_rows = residual.shape[0]
    store, me = place()
    small = [
        pltpu.make_async_copy(attention, acts, done.at[tensors]),
        pltpu.make_async_copy(residual, kept_rows, done.at[tensors + 1]),
        pltpu.make_async_copy(adapters_in, adapter_of, done.at[tensors + 2]),
        pltpu.make_async_copy(slots_in, slot_of, done.at[tensors + 3]),
    ]
    for copy in small:
        copy.start()
    copies = [
        pltpu.make_async_copy(weight.at[:, pl.ds(t * piece, piece)], held.at[t], done.at[t])
        for t in range(tensors)
    ]
    for copy in copies:
        copy.start()
    for copy in small:
        copy.wait()
    lane_slot = store * adapters + lax.broadcasted_iota(jnp.int32, (1, LANES), 1) // rank
    for r in range(stores):
        for j in range(requests):
            slot = slot_of[adapter_of[(store ^ r) * requests + j]]
            i = r * requests + j
            match[i : i + 1] = jnp.where(lane_slot == slot, 1.0, 0.0)
    row = lax.broadcasted_iota(jnp.int32, (rows, piece), 0)
    for t in range(tensors):
        kept = kept_rows[:, t * piece : (t + 1) * piece].astype(f32)
        copies[t].wait()
        total = jnp.dot(acts[...], held[t], preferred_element_type=f32)
        for i in range(sp_rows):
            total = total + jnp.where(row == me * sp_rows + i, kept[i : i + 1], 0.0)
        out[t] = total.astype(bf16)


def shrink_and_pack(stores, requests, base, match, down, *refs):
    packed, (keep, give, masks) = refs[:stores][::-1], refs[stores:]
    _, rows, piece = base.shape
    head = down.shape[1]
    pieces = []
    for r in range(stores):
        owner = packed[r][:, head:].astype(f32)
        mask = jnp.zeros((rows, LANES), f32)
        for j in range(requests):
            i = r * requests + j
            mask = mask + jnp.where(owner == j, match[i : i + 1], 0.0)
        masks[r] = mask
        pieces.append((rows_dot_rows(packed[r][:, :head], down[...]) * mask).astype(bf16))
    shrunk = jnp.concatenate(pieces, axis=1)
    me = lax.axis_index("tensor")
    for c in range(keep.shape[0]):
        for out, t in ((keep, me ^ (2 * c)), (give, me ^ (2 * c + 1))):
            out[c, :, :piece] = base[t]
            out[c, :, piece:] = shrunk


def halve(keep, got, own, *sent):
    own[...] = keep[0].astype(f32) + got[0].astype(f32)
    for c, out in enumerate(sent[::-1]):
        out[...] = (keep[c + 1].astype(f32) + got[c + 1].astype(f32)).astype(bf16)


def sum_and_raise(stores, piece, chips, up, half, *refs):
    came, (own, *sent) = refs[: chips - 1], refs[chips - 1 :]
    sent = sent[::-1]
    total = half[...]
    for c in came:
        total = total + c[...].astype(f32)
    base = total[:, :piece]
    rows = base.shape[0]
    for r in range(stores):
        shrunk = total[:, piece + r * LANES : piece + (r + 1) * LANES].astype(bf16)
        lora = adapter_factor * jnp.dot(shrunk, up[...], preferred_element_type=f32)
        if r == 0:
            own[...] = base + lora
        else:
            sent[r - 1][:rows] = base.astype(bf16)
            sent[r - 1][rows:] = lora.astype(bf16)


def hidden_and_shrink(stores, own, masks, gain, down, *refs):
    n = stores - 1
    sent, came, out = refs[:n][::-1], refs[n : 2 * n][::-1], refs[-1]
    rows, piece = own.shape
    mine = own[...]
    for r in range(n):
        mine = mine + came[r][rows:].astype(f32)
    hidden = mine.astype(bf16)
    out[:, :piece] = hidden
    gains = gain[lax.axis_index("tensor")]
    for r in range(stores):
        if r == 0:
            wide = hidden.astype(f32)
        else:
            wide = came[r - 1][:rows].astype(f32) + sent[r - 1][rows:].astype(f32)
        shrunk = rows_dot_rows((wide * gains).astype(bf16), down[...]) * masks[r]
        out[:, piece + r * LANES : piece + (r + 1) * LANES] = shrunk.astype(bf16)


def raise_queries(stores, tensors, piece, up, *refs):
    blocks, out = refs[:tensors], refs[tensors:]
    out = out[:1] + out[:0:-1]
    for r in range(stores):
        columns = slice(piece + r * LANES, piece + (r + 1) * LANES)
        shrunk = blocks[0][:, columns].astype(f32)
        for block in blocks[1:]:
            shrunk = shrunk + block[:, columns].astype(f32)
        raised = adapter_factor * jnp.dot(shrunk.astype(bf16), up[...], preferred_element_type=f32)
        out[r][...] = raised.astype(out[r].dtype)


def base_queries(tensors, gain, weight, raised, *refs):
    blocks, (hidden, base, scale) = refs[:tensors], refs[tensors:]
    sp_rows, width = hidden.shape
    piece = width // tensors
    rows = base.shape[0]
    me = lax.axis_index("tensor")
    total = jnp.zeros(base.shape, f32)
    squares = jnp.zeros((rows, 1), f32)
    row = lax.broadcasted_iota(jnp.int32, (rows, piece), 0)
    for i in range(tensors):
        k = me ^ i
        at = pl.multiple_of(k * piece, piece)
        wide = blocks[i][:, :piece].astype(f32)
        squares = squares + jnp.sum(wide * wide, axis=1, keepdims=True)
        total = total + jnp.dot(
            (wide * gain[k]).astype(bf16), weight[pl.ds(at, piece)], preferred_element_type=f32
        )
        picked = [
            jnp.sum(jnp.where(row == me * sp_rows + j, wide, 0.0), axis=0, keepdims=True)
            for j in range(sp_rows)
        ]
        hidden[:, pl.ds(at, piece)] = jnp.concatenate(picked, axis=0).astype(bf16)
    s = jnp.broadcast_to(lax.rsqrt(squares / width + 1e-05), base.shape)
    scale[...] = s
    base[...] = s * (total + raised[...])


def on_device(
    attention_output,
    residual_input,
    output_weight,
    query_weight,
    next_norm_gain,
    output_down_maps,
    output_up_maps,
    query_down_maps,
    query_up_maps,
    request_adapter,
    adapter_store_slot,
    request_block_count,
):
    stores, tensors = lax.axis_size("store"), lax.axis_size("tensor")
    rows, head = attention_output.shape
    sp_rows, width = residual_input.shape
    requests = request_block_count.shape[1]
    adapters, _, rank = output_down_maps.shape
    piece = output_up_maps.shape[2]
    queries_here = query_weight.shape[1]
    pairs, chips = adapters * rank, tensors // 2
    down_o = output_down_maps.transpose(0, 2, 1).reshape(pairs, head)
    up_o = output_up_maps.reshape(pairs, piece)
    down_q = query_down_maps.transpose(0, 2, 1).reshape(pairs, piece)
    up_q = query_up_maps.reshape(pairs, queries_here)
    gain = next_norm_gain.reshape(tensors, 1, piece)
    message = piece + stores * LANES

    def swap(a, axis, bits):
        return lax.ppermute(a, axis, [(i, i ^ bits) for i in range(lax.axis_size(axis))])

    def kernel(body, out, name, in_specs, **kw):
        return pl.pallas_call(
            body,
            out_shape=[jax.ShapeDtypeStruct(*o) for o in out],
            in_specs=in_specs,
            out_specs=[VMEM] * len(out),
            name=name,
            compiler_params=params(),
            **kw,
        )

    def stay(a):
        return pltpu.with_memory_space_constraint(a, pltpu.HBM)

    [packed0] = kernel(
        functools.partial(pack_rows, requests, sp_rows),
        [((rows, head + LANES), bf16)],
        "pack_rows",
        [HBM, HBM],
        scratch_shapes=[
            pltpu.SMEM((1, requests), jnp.int32),
            pltpu.VMEM((rows, head), bf16),
            pltpu.SemaphoreType.DMA((2,)),
        ],
    )(stay(request_block_count), stay(attention_output))
    packed = [packed0] + [swap(packed0, "store", r) for r in range(1, stores)]

    base, match = kernel(
        functools.partial(base_rows, stores, requests, adapters, rank),
        [((tensors, rows, piece), bf16), ((stores * requests, LANES), f32)],
        "base_rows",
        [HBM] * 5,
        scratch_shapes=[
            pltpu.SMEM(request_adapter.shape, jnp.int32),
            pltpu.SMEM(adapter_store_slot.shape, jnp.int32),
            pltpu.VMEM((rows, head), bf16),
            pltpu.VMEM((sp_rows, width), bf16),
            pltpu.VMEM((tensors, head, piece), bf16),
            pltpu.SemaphoreType.DMA((tensors + 4,)),
        ],
        cost_estimate=pl.CostEstimate(
            flops=2 * rows * head * width, bytes_accessed=2 * head * width, transcendentals=0
        ),
    )(
        stay(request_adapter),
        stay(adapter_store_slot),
        stay(attention_output),
        stay(output_weight),
        stay(residual_input),
    )

    keep, give, masks = kernel(
        functools.partial(shrink_and_pack, stores, requests),
        [((chips, rows, message), bf16)] * 2 + [((stores, rows, LANES), f32)],
        "shrink_and_pack",
        [VMEM] * (3 + stores),
    )(base, match, down_o, *packed[::-1])
    got = swap(give, "tensor", 1)
    half, *halves = kernel(
        halve,
        [((rows, message), f32)] + [((rows, message), bf16)] * (chips - 1),
        "halve",
        [VMEM] * 2,
    )(keep, got)
    pieces = [swap(h, "tensor", 2 * (c + 1)) for c, h in enumerate(halves[::-1])]

    own, *sent = kernel(
        functools.partial(sum_and_raise, stores, piece, chips),
        [((rows, piece), f32)] + [((2 * rows, piece), bf16)] * (stores - 1),
        "sum_and_raise",
        [VMEM] * (1 + chips),
    )(up_o, half, *pieces[::-1])
    sent = sent[::-1]
    came = [swap(a, "store", r + 1) for r, a in enumerate(sent)]

    [mine] = kernel(
        functools.partial(hidden_and_shrink, stores),
        [((rows, message), bf16)],
        "hidden_and_shrink",
        [VMEM] * (4 + 2 * (stores - 1)),
    )(own, masks, gain, down_q, *sent[::-1], *came[::-1])
    even = [mine] + [swap(mine, "tensor", 2 * c) for c in range(1, chips)]
    blocks = [b for e in even for b in (e, swap(e, "tensor", 1))]

    raised, *back = kernel(
        functools.partial(raise_queries, stores, tensors, piece),
        [((rows, queries_here), f32)] + [((rows, queries_here), bf16)] * (stores - 1),
        "raise_queries",
        [VMEM] * (1 + tensors),
    )(up_q, *blocks)
    returned = [swap(a, "store", r + 1) for r, a in enumerate(back[::-1])]

    new_hidden, base_q, scale = kernel(
        functools.partial(base_queries, tensors),
        [((sp_rows, width), bf16)] + [((rows, queries_here), f32)] * 2,
        "base_queries",
        [VMEM] * (3 + tensors),
        cost_estimate=pl.CostEstimate(
            flops=2 * rows * width * queries_here,
            bytes_accessed=2 * width * queries_here,
            transcendentals=0,
        ),
    )(gain, query_weight, raised, *blocks)
    queries = base_q + scale * sum(a.astype(f32) for a in returned[::-1])
    return new_hidden, queries.astype(bf16)


def solution(mesh):
    in_specs = (
        P("store", "tensor"),
        P(("store", "tensor"), None),
        P("tensor", None),
        P(None, "tensor"),
        P(),
        P("store", "tensor", None),
        P("store", None, "tensor"),
        P("store", "tensor", None),
        P("store", None, "tensor"),
        P(),
        P(),
        P("store", None),
    )
    out_specs = (P(("store", "tensor"), None), P("store", "tensor"))
    return jax.shard_map(
        on_device, mesh=mesh, in_specs=in_specs, out_specs=out_specs, check_vma=False
    )
```

```python
import functools

import jax
import jax.numpy as jnp
from jax import lax
from jax.experimental import pallas as pl
from jax.experimental.pallas import tpu as pltpu
from jax.sharding import PartitionSpec as P

adapter_factor = 0.5
LANES = 128
SMEM = pl.BlockSpec(memory_space=pltpu.SMEM)
VMEM = pl.BlockSpec(memory_space=pltpu.VMEM)
HBM = pl.BlockSpec(memory_space=pltpu.HBM)
bf16, f32 = jnp.bfloat16, jnp.float32


def params(**kw):
    return pltpu.CompilerParams(vmem_limit_bytes=48 * 2**20, **kw)


def rows_dot_rows(a, b):
    return lax.dot_general(a, b, (((1,), (1,)), ((), ())), preferred_element_type=f32)


def place():
    return lax.axis_index("store"), lax.axis_index("tensor")


def pack_rows(requests, sp_rows, counts, attention, out, count, loaded, done):
    first = pltpu.make_async_copy(counts, count, done.at[0])
    second = pltpu.make_async_copy(attention, loaded, done.at[1])
    first.start()
    second.start()
    rows, head = loaded.shape
    row = lax.broadcasted_iota(jnp.int32, (rows, LANES), 0)
    owner = jnp.zeros((rows, LANES), f32)
    first.wait()
    end = jnp.int32(0)
    for j in range(requests - 1):
        end = end + count[0, j] * sp_rows
        owner = owner + jnp.where(row >= end, 1.0, 0.0)
    out[:, head:] = owner.astype(bf16)
    second.wait()
    out[:, :head] = loaded[...]


def fold(a, adapters):
    rank = a.shape[1] // adapters
    return sum(a[:, i * rank : (i + 1) * rank] for i in range(adapters))


def unfold(a, adapters, mask):
    return jnp.concatenate([a] * adapters, axis=1) * mask


def base_rows(
    stores, requests, adapters, rank, adapters_in, slots_in, attention, weight, residual,
    out, match, adapter_of, slot_of, acts, kept_rows, held, done,
):
    tensors, rows, piece = out.shape
    sp_rows = residual.shape[0]
    store, me = place()
    small = [
        pltpu.make_async_copy(attention, acts, done.at[tensors]),
        pltpu.make_async_copy(residual, kept_rows, done.at[tensors + 1]),
        pltpu.make_async_copy(adapters_in, adapter_of, done.at[tensors + 2]),
        pltpu.make_async_copy(slots_in, slot_of, done.at[tensors + 3]),
    ]
    for copy in small:
        copy.start()
    copies = [
        pltpu.make_async_copy(weight.at[:, pl.ds(t * piece, piece)], held.at[t], done.at[t])
        for t in range(tensors)
    ]
    for copy in copies:
        copy.start()
    for copy in small:
        copy.wait()
    lane_slot = store * adapters + lax.broadcasted_iota(jnp.int32, (1, LANES), 1) // rank
    for r in range(stores):
        for j in range(requests):
            slot = slot_of[adapter_of[(store ^ r) * requests + j]]
            i = r * requests + j
            match[i : i + 1] = jnp.where(lane_slot == slot, 1.0, 0.0)
    row = lax.broadcasted_iota(jnp.int32, (rows, piece), 0)
    for t in range(tensors):
        kept = kept_rows[:, t * piece : (t + 1) * piece].astype(f32)
        copies[t].wait()
        total = jnp.dot(acts[...], held[t], preferred_element_type=f32)
        for i in range(sp_rows):
            total = total + jnp.where(row == me * sp_rows + i, kept[i : i + 1], 0.0)
        out[t] = total.astype(bf16)


def shrink_and_pack(stores, requests, adapters, base, match, down, *refs):
    packed, (keep, give, masks) = refs[:stores][::-1], refs[stores:]
    _, rows, piece = base.shape
    head = down.shape[1]
    pieces = []
    for r in range(stores):
        owner = packed[r][:, head:].astype(f32)
        mask = jnp.zeros((rows, LANES), f32)
        for j in range(requests):
            i = r * requests + j
            mask = mask + jnp.where(owner == j, match[i : i + 1], 0.0)
        masks[r] = mask
        pieces.append(fold(rows_dot_rows(packed[r][:, :head], down[...]) * mask, adapters))
    shrunk = jnp.concatenate(pieces, axis=1).astype(bf16)
    me = lax.axis_index("tensor")
    for c in range(keep.shape[0]):
        for out, t in ((keep, me ^ (2 * c)), (give, me ^ (2 * c + 1))):
            out[c, :, :piece] = base[t]
            out[c, :, piece:] = shrunk


def halve(keep, got, own, *sent):
    own[...] = keep[0].astype(f32) + got[0].astype(f32)
    for c, out in enumerate(sent[::-1]):
        out[...] = (keep[c + 1].astype(f32) + got[c + 1].astype(f32)).astype(bf16)


def sum_and_raise(stores, adapters, piece, chips, masks, up, half, *refs):
    came, (own, *sent) = refs[: chips - 1], refs[chips - 1 :]
    sent = sent[::-1]
    total = half[...]
    for c in came:
        total = total + c[...].astype(f32)
    base = total[:, :piece]
    rows, rank = base.shape[0], up.shape[0] // adapters
    for r in range(stores):
        shrunk = total[:, piece + r * rank : piece + (r + 1) * rank]
        shrunk = unfold(shrunk, adapters, masks[r]).astype(bf16)
        lora = adapter_factor * jnp.dot(shrunk, up[...], preferred_element_type=f32)
        if r == 0:
            own[...] = base + lora
        else:
            sent[r - 1][:rows] = base.astype(bf16)
            sent[r - 1][rows:] = lora.astype(bf16)


def hidden_and_shrink(stores, adapters, own, masks, gain, down, *refs):
    n = stores - 1
    sent, came, out = refs[:n], refs[n : 2 * n], refs[-1]
    sent, came = sent[-1:] + sent[:-1], came[-1:] + came[:-1]
    rows, piece = own.shape
    mine = own[...]
    for r in range(n):
        mine = mine + came[r][rows:].astype(f32)
    hidden = mine.astype(bf16)
    out[:, :piece] = hidden
    gains = gain[lax.axis_index("tensor")]
    pieces = []
    for r in range(stores):
        if r == 0:
            wide = hidden.astype(f32)
        else:
            wide = came[r - 1][:rows].astype(f32) + sent[r - 1][rows:].astype(f32)
        shrunk = rows_dot_rows((wide * gains).astype(bf16), down[...]) * masks[r]
        pieces.append(fold(shrunk, adapters))
    out[:, piece:] = jnp.concatenate(pieces, axis=1).astype(bf16)


def raise_queries(stores, adapters, tensors, piece, masks, up, *refs):
    blocks, out = refs[:tensors], refs[tensors:]
    out = out[:1] + out[:0:-1]
    rank = up.shape[0] // adapters
    for r in range(stores):
        columns = slice(piece + r * rank, piece + (r + 1) * rank)
        shrunk = blocks[0][:, columns].astype(f32)
        for block in blocks[1:]:
            shrunk = shrunk + block[:, columns].astype(f32)
        shrunk = unfold(shrunk, adapters, masks[r])
        raised = adapter_factor * jnp.dot(shrunk.astype(bf16), up[...], preferred_element_type=f32)
        out[r][...] = raised.astype(out[r].dtype)


def base_queries(tensors, gain, weight, raised, *refs):
    blocks, (hidden, base, scale) = refs[:tensors], refs[tensors:]
    sp_rows, width = hidden.shape
    piece = width // tensors
    rows = base.shape[0]
    me = lax.axis_index("tensor")
    total = jnp.zeros(base.shape, f32)
    squares = jnp.zeros((rows, 1), f32)
    row = lax.broadcasted_iota(jnp.int32, (rows, piece), 0)
    for i in range(tensors):
        k = me ^ i
        at = pl.multiple_of(k * piece, piece)
        wide = blocks[i][:, :piece].astype(f32)
        squares = squares + jnp.sum(wide * wide, axis=1, keepdims=True)
        total = total + jnp.dot(
            (wide * gain[k]).astype(bf16), weight[pl.ds(at, piece)], preferred_element_type=f32
        )
        picked = [
            jnp.sum(jnp.where(row == me * sp_rows + j, wide, 0.0), axis=0, keepdims=True)
            for j in range(sp_rows)
        ]
        hidden[:, pl.ds(at, piece)] = jnp.concatenate(picked, axis=0).astype(bf16)
    s = jnp.broadcast_to(lax.rsqrt(squares / width + 1e-05), base.shape)
    scale[...] = s
    base[...] = s * (total + raised[...])


def on_device(
    attention_output,
    residual_input,
    output_weight,
    query_weight,
    next_norm_gain,
    output_down_maps,
    output_up_maps,
    query_down_maps,
    query_up_maps,
    request_adapter,
    adapter_store_slot,
    request_block_count,
):
    stores, tensors = lax.axis_size("store"), lax.axis_size("tensor")
    rows, head = attention_output.shape
    sp_rows, width = residual_input.shape
    requests = request_block_count.shape[1]
    adapters, _, rank = output_down_maps.shape
    piece = output_up_maps.shape[2]
    queries_here = query_weight.shape[1]
    pairs, chips = adapters * rank, tensors // 2
    down_o = output_down_maps.transpose(0, 2, 1).reshape(pairs, head)
    up_o = output_up_maps.reshape(pairs, piece)
    down_q = query_down_maps.transpose(0, 2, 1).reshape(pairs, piece)
    up_q = query_up_maps.reshape(pairs, queries_here)
    gain = next_norm_gain.reshape(tensors, 1, piece)
    message = piece + stores * rank

    def swap(a, axis, bits):
        return lax.ppermute(a, axis, [(i, i ^ bits) for i in range(lax.axis_size(axis))])

    def kernel(body, out, name, in_specs, **kw):
        return pl.pallas_call(
            body,
            out_shape=[jax.ShapeDtypeStruct(*o) for o in out],
            in_specs=in_specs,
            out_specs=[VMEM] * len(out),
            name=name,
            compiler_params=params(),
            **kw,
        )

    def stay(a):
        return pltpu.with_memory_space_constraint(a, pltpu.HBM)

    [packed0] = kernel(
        functools.partial(pack_rows, requests, sp_rows),
        [((rows, head + LANES), bf16)],
        "pack_rows",
        [HBM, HBM],
        scratch_shapes=[
            pltpu.SMEM((1, requests), jnp.int32),
            pltpu.VMEM((rows, head), bf16),
            pltpu.SemaphoreType.DMA((2,)),
        ],
    )(stay(request_block_count), stay(attention_output))
    packed = [packed0] + [swap(packed0, "store", r) for r in range(1, stores)]

    base, match = kernel(
        functools.partial(base_rows, stores, requests, adapters, rank),
        [((tensors, rows, piece), bf16), ((stores * requests, LANES), f32)],
        "base_rows",
        [HBM] * 5,
        scratch_shapes=[
            pltpu.SMEM(request_adapter.shape, jnp.int32),
            pltpu.SMEM(adapter_store_slot.shape, jnp.int32),
            pltpu.VMEM((rows, head), bf16),
            pltpu.VMEM((sp_rows, width), bf16),
            pltpu.VMEM((tensors, head, piece), bf16),
            pltpu.SemaphoreType.DMA((tensors + 4,)),
        ],
        cost_estimate=pl.CostEstimate(
            flops=2 * rows * head * width, bytes_accessed=2 * head * width, transcendentals=0
        ),
    )(
        stay(request_adapter),
        stay(adapter_store_slot),
        stay(attention_output),
        stay(output_weight),
        stay(residual_input),
    )

    keep, give, masks = kernel(
        functools.partial(shrink_and_pack, stores, requests, adapters),
        [((chips, rows, message), bf16)] * 2 + [((stores, rows, LANES), f32)],
        "shrink_and_pack",
        [VMEM] * (3 + stores),
    )(base, match, down_o, *packed[::-1])
    got = swap(give, "tensor", 1)
    half, *halves = kernel(
        halve,
        [((rows, message), f32)] + [((rows, message), bf16)] * (chips - 1),
        "halve",
        [VMEM] * 2,
    )(keep, got)
    pieces = [swap(h, "tensor", 2 * (c + 1)) for c, h in enumerate(halves[::-1])]

    own, *sent = kernel(
        functools.partial(sum_and_raise, stores, adapters, piece, chips),
        [((rows, piece), f32)] + [((2 * rows, piece), bf16)] * (stores - 1),
        "sum_and_raise",
        [VMEM] * (2 + chips),
    )(masks, up_o, half, *pieces[::-1])
    sent = sent[::-1]
    came = [swap(a, "store", r + 1) for r, a in enumerate(sent)]

    [mine] = kernel(
        functools.partial(hidden_and_shrink, stores, adapters),
        [((rows, message), bf16)],
        "hidden_and_shrink",
        [VMEM] * (4 + 2 * (stores - 1)),
    )(own, masks, gain, down_q, *sent[1:], sent[0], *came[1:], came[0])
    even = [mine] + [swap(mine, "tensor", 2 * c) for c in range(1, chips)]
    blocks = [b for e in even for b in (e, swap(e, "tensor", 1))]

    raised, *back = kernel(
        functools.partial(raise_queries, stores, adapters, tensors, piece),
        [((rows, queries_here), f32)] + [((rows, queries_here), bf16)] * (stores - 1),
        "raise_queries",
        [VMEM] * (2 + tensors),
    )(masks, up_q, *blocks)
    returned = [swap(a, "store", r + 1) for r, a in enumerate(back[::-1])]

    new_hidden, base_q, scale = kernel(
        functools.partial(base_queries, tensors),
        [((sp_rows, width), bf16)] + [((rows, queries_here), f32)] * 2,
        "base_queries",
        [VMEM] * (3 + tensors),
        cost_estimate=pl.CostEstimate(
            flops=2 * rows * width * queries_here,
            bytes_accessed=2 * width * queries_here,
            transcendentals=0,
        ),
    )(gain, query_weight, raised, *blocks)
    queries = base_q + scale * sum(a.astype(f32) for a in returned[::-1])
    return new_hidden, queries.astype(bf16)


def solution(mesh):
    in_specs = (
        P("store", "tensor"),
        P(("store", "tensor"), None),
        P("tensor", None),
        P(None, "tensor"),
        P(),
        P("store", "tensor", None),
        P("store", None, "tensor"),
        P("store", "tensor", None),
        P("store", None, "tensor"),
        P(),
        P(),
        P("store", None),
    )
    out_specs = (P(("store", "tensor"), None), P("store", "tensor"))
    return jax.shard_map(
        on_device, mesh=mesh, in_specs=in_specs, out_specs=out_specs, check_vma=False
    )
```
